512 devices in a mesh: blk: 64 (over z_lo, x, core), feat: 8 (over z_hi, y).
Axes of the slice: x: 4, y: 4, z: 16 (z_hi: 2, z_lo: 8; z = z_hi * 8 + z_lo), core: 2. Of those that a mesh axis runs over, the one named last changes fastest.
Arguments:
- grads: bfloat16 [32768, 16384], P('blk', 'feat'), may hold values from -6 to 6
- basis_left: float32 [8, 16, 16], P('feat'), may hold values from -1.5 to 1.5
- basis_right: float32 [8, 128, 128], P('feat'), may hold values from -0.5 to 0.5
- eigen: float32 [16384], P('feat'), may hold values from 0.05 to 20
- partner: int32 [1, 64], replicated, may hold values from 0 to 63, as said below
Outputs:
- tiles: float32 [1, 32768, 512], P(None, 'blk', 'feat')
The draws below stay inside these ranges and needn't reach their ends.
Inputs may be any that keep to these rules, and one draw needn't show every extreme that they name: In every round partner[r, b] = b xor 2^k_r, one bit k_r per round, distinct between rounds; so the partners form a perfect matching.
All inputs are finite; a program needn't handle non-finite values.
Results may differ from the reference program's by a relative error of at most 0.0029.
Values may be sent and summed in bfloat16 or wider, within the bound.
No kernel may reach another device: no remote copies, remote signals or barrier semaphores. Data moves between devices by JAX's collectives and lax.ppermute only.
A program may use at most 64 MiB of HBM per device.

```python
import math
import jax
import jax.numpy as jnp
from jax import lax

F = 16384
FA = 16
FB = 128
LB = 8
EX = 512
ROUNDS = 1
EXAMPLES = 32768
N_BLK = 64


def draw_partner(key, part):
    key = jax.random.fold_in(key, 11)
    levels = N_BLK.bit_length() - 1
    chosen = jax.random.permutation(key, levels).astype(jnp.int32)
    masks = jnp.left_shift(jnp.int32(1), chosen[:ROUNDS])
    owners = jnp.arange(N_BLK, dtype=jnp.int32)
    return jnp.bitwise_xor(owners[None, :], masks[:, None]).astype(jnp.int32)


def block_scale(rng, shape, pieces, smallest, top_value):
    gain = 1.0
    for position, shards_of in pieces:
        heights = jax.random.uniform(jax.random.fold_in(jax.random.fold_in(rng, 6), position), (shards_of,), jnp.float32, smallest / len(pieces), top_value / len(pieces))
        gain = gain * jnp.repeat(jnp.exp(heights), shape[position] // shards_of).reshape((-1,) + (1,) * (len(shape) - 1 - position))
    return gain


def scatter_about(rng, dims, scale, reach, cuts=(), kind=jnp.bfloat16):
    entries = jax.random.normal(rng, dims, jnp.float32) * scale
    if len(cuts) > 0:
        entries = block_scale(rng, dims, cuts, -0.22, 0.18) * entries
    return jnp.clip(entries, min=-reach, max=reach).astype(kind)


def setup_inputs(seed: int = 0) -> dict:
    seeds = jax.random.split(jax.random.key(seed), 6)
    grads = scatter_about(seeds[0], (EXAMPLES, F), 1.0, 6.0, ((0, 64), (1, 8)))
    basis_left = scatter_about(seeds[1], (LB, FA, FA), FA ** -0.5, 1.5, ((0, 8),), jnp.float32)
    basis_right = scatter_about(seeds[2], (LB, FB, FB), FB ** -0.5, 0.5, ((0, 8),), jnp.float32)
    eigen = jnp.clip(jnp.exp(math.log(20.0) - 5.9914645 * jax.random.uniform(seeds[3], (F,), jnp.float32) ** block_scale(seeds[3], (F,), ((0, 8),), -0.2, 0.2)), 0.05, 20.0)
    partner = draw_partner(jax.random.fold_in(seeds[5], 71), 0)
    return {"grads": grads, "basis_left": basis_left, "basis_right": basis_right, "eigen": eigen, "partner": partner}


precision_high = lax.Precision.HIGHEST

def precondition(rows, basis_left, basis_right, eigen):
    row_count = rows.shape[0]
    layer_count = basis_left.shape[0]
    reshaped = rows.astype(jnp.float32).reshape(row_count, layer_count, basis_left.shape[1], basis_right.shape[1])
    damped = eigen.reshape(layer_count, basis_left.shape[1], basis_right.shape[1]) + 0.1
    sectioned = jnp.einsum('elab,lbd->elad', reshaped, basis_right, precision=precision_high)
    rotated = jnp.einsum('elad,lac->elcd', sectioned, basis_left, precision=precision_high) / damped[None]
    sectioned = jnp.einsum('elcd,lac->elad', rotated, basis_left, precision=precision_high)
    restored = jnp.einsum('elad,lbd->elab', sectioned, basis_right, precision=precision_high)
    return restored.reshape(row_count, -1).astype(jnp.bfloat16)

def reference(grads, basis_left, basis_right, eigen, partner):
    owners = grads.reshape(N_BLK, EX, F)
    precond = lax.map(lambda rows: precondition(rows, basis_left, basis_right, eigen), owners)
    scaling = 1.0 / jnp.sqrt(jnp.float32(F))
    results = []
    for round_index in range(ROUNDS):

        def one_owner(owner_id):
            opposite = partner[round_index, owner_id]
            is_lower = owner_id < opposite
            left_rows = jnp.where(is_lower, precond[owner_id], owners[owner_id])
            right_rows = jnp.where(is_lower, owners[opposite], precond[opposite])
            product = lax.dot_general(left_rows, right_rows, (((1,), (1,)), ((), ())), preferred_element_type=jnp.float32)
            return product * scaling
        tile_set = lax.map(one_owner, jnp.arange(N_BLK, dtype=jnp.int32))
        results.append(tile_set.reshape(N_BLK * EX, EX))
    return jnp.stack(results)
```

```python
import functools

import jax
import jax.numpy as jnp
from jax import lax
from jax.experimental import pallas as pl
from jax.experimental.pallas import tpu as pltpu
from jax.sharding import PartitionSpec as P

FEATURES = 16384
FA = 16
FB = 128
ROWS = 512
COLS = FA * FB
WIDE = 16 * FA
Y_GROUPS = [[0, 1, 2, 3], [4, 5, 6, 7]]
VMEM = pl.BlockSpec(memory_space=pltpu.VMEM)
SMEM = pl.BlockSpec(memory_space=pltpu.SMEM)
f32, bf16 = jnp.float32, jnp.bfloat16


def split(v):
    high = v.astype(bf16)
    return high, (v - high.astype(f32)).astype(bf16)


def dot(a, b):
    return jnp.dot(a, b, preferred_element_type=f32)


def dot_t(a, b):
    return lax.dot_general(a, b, (((1,), (1,)), ((), ())), preferred_element_type=f32)


def prepare(left, right, damped, lt, l, rs, rr, inv):
    spread = (
        lax.broadcasted_iota(jnp.int32, (WIDE, FA), 0) >> 4
        == lax.broadcasted_iota(jnp.int32, (WIDE, FA), 1)
    ).astype(bf16)
    same = (lax.broadcasted_iota(jnp.int32, (WIDE, WIDE), 0) & 15) == (
        lax.broadcasted_iota(jnp.int32, (WIDE, WIDE), 1) & 15
    )
    for k, v in enumerate(split(left[...])):
        wide = dot_t(dot(spread, v).astype(bf16), spread)
        l[k] = jnp.where(same, wide, 0.0).astype(bf16)
        wide = dot_t(dot_t(spread, v).astype(bf16), spread)
        lt[k] = jnp.where(same, wide, 0.0).astype(bf16)
    basis = right[...]
    for k, v in enumerate(split(basis)):
        rs[:, k * FB : (k + 1) * FB] = v
    for k, v in enumerate(split(basis.T)):
        rr[:FB, k * FB : (k + 1) * FB] = v
        rr[FB:, k * FB : (k + 1) * FB] = v
    reciprocal = 1.0 / (damped[...] + 0.1)
    inv[...] = jnp.broadcast_to(reciprocal[:, None, :], (FA, 16, FB)).reshape(WIDE, FB)


PREPARED = (
    jax.ShapeDtypeStruct((2, WIDE, WIDE), bf16),
    jax.ShapeDtypeStruct((2, WIDE, WIDE), bf16),
    jax.ShapeDtypeStruct((FB, 2 * FB), bf16),
    jax.ShapeDtypeStruct((2 * FB, 2 * FB), bf16),
    jax.ShapeDtypeStruct((WIDE, FB), f32),
)


def prepared(left, right, damped):
    return pl.pallas_call(
        prepare, out_shape=PREPARED, in_specs=[VMEM] * 3, out_specs=[VMEM] * 5, name="prepare"
    )(left, right, damped)


def halves(v):
    return v[:, :FB] + v[:, FB:]


def precondition(x, out, lt, l, rs, rr, inv):
    def group(g, carry):
        at = pl.ds(pl.multiple_of(g * 16, 16), 16)
        z = jnp.concatenate([x[at, a * FB : (a + 1) * FB] for a in range(FA)], axis=0)
        v = halves(dot(z, rs[...]))
        high, low = split(v)
        v = halves(dot(lt[0], jnp.concatenate([high, low], axis=1))) + dot(lt[1], high)
        high, low = split(v * inv[...])
        v = halves(dot(l[0], jnp.concatenate([high, low], axis=1))) + dot(l[1], high)
        high, low = split(v)
        v = halves(dot(jnp.concatenate([high, low], axis=1), rr[...])).astype(bf16)
        for a in range(FA):
            out[at, a * FB : (a + 1) * FB] = v[a * 16 : (a + 1) * 16]
        return carry

    lax.fori_loop(0, x.shape[0] // 16, group, 0, unroll=2)


def own_kernel(lower, x, lt, l, rs, rr, inv, out):
    @pl.when(lower[0] == 1)
    def _():
        precondition(x, out, lt, l, rs, rr, inv)

    @pl.when(lower[0] == 0)
    def _():
        out[...] = x[...]


def whole(a):
    return pl.BlockSpec(a.shape, lambda i: (0,) * len(a.shape))


def own_side(lower, x, ready, step=128):
    rows = pl.BlockSpec((step, COLS), lambda i: (i, 0))
    return pl.pallas_call(
        own_kernel,
        grid=(x.shape[0] // step,),
        out_shape=jax.ShapeDtypeStruct(x.shape, bf16),
        in_specs=[SMEM, rows] + [whole(a) for a in ready],
        out_specs=rows,
        name="own",
    )(lower, x, *ready)


def tile_kernel(lower, y, own, lt, l, rs, rr, inv, out, held):
    @pl.when(lower[0] == 1)
    def _():
        out[0, 0] = dot_t(y[...], own[...]) * (1.0 / 128.0)

    @pl.when(lower[0] == 0)
    def _():
        precondition(y, held, lt, l, rs, rr, inv)
        out[0, 0] = dot_t(held[...], own[...]) * (1.0 / 128.0)


def tile_side(lower, y, own, ready):
    step = y.shape[0] // 8
    return pl.pallas_call(
        tile_kernel,
        grid=(8,),
        out_shape=jax.ShapeDtypeStruct((4, 2, step, ROWS), f32),
        in_specs=[SMEM, pl.BlockSpec((step, COLS), lambda i: (i, 0)), whole(own)]
        + [whole(a) for a in ready],
        out_specs=pl.BlockSpec((1, 1, step, ROWS), lambda i: (i % 4, i // 4, 0, 0)),
        scratch_shapes=[pltpu.VMEM((step, COLS), bf16)],
        name="tile",
    )(lower, y, own, *ready)


def fold_kernel(z_hi, parts, keep, send):
    z = z_hi[0]
    keep[...] = parts[0, z] + parts[1, z] + parts[2, z] + parts[3, z]
    o = 1 - z
    send[...] = (parts[0, o] + parts[1, o] + parts[2, o] + parts[3, o]).astype(send.dtype)


def fold(z_hi, parts):
    shape = parts.shape[2:]
    return pl.pallas_call(
        fold_kernel,
        out_shape=(jax.ShapeDtypeStruct(shape, f32), jax.ShapeDtypeStruct(shape, f32)),
        in_specs=[SMEM, VMEM],
        out_specs=(VMEM, VMEM),
        name="fold",
    )(z_hi, parts)


def summed(z_hi, tile):
    parts = lax.all_to_all(tile, "feat", 0, 0, axis_index_groups=Y_GROUPS)
    keep, send = fold(z_hi, parts)
    return keep + lax.ppermute(send, "feat", [(f, f ^ 4) for f in range(8)])


def swap(level, x):
    return lax.ppermute(x, "blk", [(b, b ^ (1 << level)) for b in range(64)])


def plain(level, x, ready, lower, z_hi):
    incoming = swap(level, x)
    own = own_side(lower, x, ready)
    return summed(z_hi, tile_side(lower, incoming, own, ready))


def body(grads, basis_left, basis_right, eigen, partner):
    mask = partner[0, 0]
    lower = (jnp.bitwise_and(lax.axis_index("blk"), mask) == 0).astype(jnp.int32).reshape(1)
    z_hi = (lax.axis_index("feat") // 4).astype(jnp.int32).reshape(1)
    level = sum((mask >= 1 << k).astype(jnp.int32) for k in range(1, 6))
    ready = prepared(basis_left[0], basis_right[0], eigen.reshape(FA, FB))
    branches = [functools.partial(plain, k) for k in range(6)]
    out = lax.switch(level, branches, grads, ready, lower, z_hi)
    return out.T[None]


def solution(mesh):
    placed = (P("blk", "feat"), P("feat", None, None), P("feat", None, None), P("feat"), P())
    return jax.shard_map(
        body, mesh=mesh, in_specs=placed, out_specs=P(None, "blk", "feat"), check_vma=False
    )
```

```python
import functools

import jax
import jax.numpy as jnp
from jax import lax
from jax.experimental import pallas as pl
from jax.experimental.pallas import tpu as pltpu
from jax.sharding import PartitionSpec as P

FA = 16
FB = 128
ROWS = 512
COLS = FA * FB
WIDE = 16 * FA
SHARE = 64
PAIRS = 4
SCALE = 1.0 / 128.0
Y_GROUPS = [[0, 1, 2, 3], [4, 5, 6, 7]]
VMEM = pl.BlockSpec(memory_space=pltpu.VMEM)
SMEM = pl.BlockSpec(memory_space=pltpu.SMEM)
ANY = pl.BlockSpec(memory_space=pl.ANY)
f32, bf16 = jnp.float32, jnp.bfloat16


def params(flops, moved):
    return dict(
        compiler_params=pltpu.CompilerParams(vmem_limit_bytes=28 << 20),
        cost_estimate=pl.CostEstimate(flops=flops, bytes_accessed=moved, transcendentals=0),
    )


def split(v):
    high = v.astype(bf16)
    return high, (v - high.astype(f32)).astype(bf16)


def dot(a, b):
    return jnp.dot(a, b, preferred_element_type=f32)


def dot_t(a, b):
    return lax.dot_general(a, b, (((1,), (1,)), ((), ())), preferred_element_type=f32)


def prepare(left, right, eigen, lt, l, rr, rrt, inv):
    spread = (
        lax.broadcasted_iota(jnp.int32, (WIDE, FA), 0) >> 4
        == lax.broadcasted_iota(jnp.int32, (WIDE, FA), 1)
    ).astype(bf16)
    same = (lax.broadcasted_iota(jnp.int32, (WIDE, WIDE), 0) & 15) == (
        lax.broadcasted_iota(jnp.int32, (WIDE, WIDE), 1) & 15
    )
    for k, v in enumerate(split(left[...])):
        wide = dot_t(dot(spread, v).astype(bf16), spread)
        l[k] = jnp.where(same, wide, 0.0).astype(bf16)
        wide = dot_t(dot_t(spread, v).astype(bf16), spread)
        lt[k] = jnp.where(same, wide, 0.0).astype(bf16)
    for out, basis in ((rr, right[...]), (rrt, right[...].T)):
        for k, v in enumerate(split(basis)):
            out[:FB, k * FB : (k + 1) * FB] = v
            out[FB:, k * FB : (k + 1) * FB] = v
    reciprocal = 1.0 / (eigen[...] + 0.1)
    inv[...] = jnp.broadcast_to(reciprocal[:, None, :], (FA, 16, FB)).reshape(WIDE, FB)


PREPARED = (
    jax.ShapeDtypeStruct((2, WIDE, WIDE), bf16),
    jax.ShapeDtypeStruct((2, WIDE, WIDE), bf16),
    jax.ShapeDtypeStruct((2 * FB, 2 * FB), bf16),
    jax.ShapeDtypeStruct((2 * FB, 2 * FB), bf16),
    jax.ShapeDtypeStruct((WIDE, FB), f32),
)


def prepared(left, right, eigen):
    return pl.pallas_call(
        prepare, out_shape=PREPARED, in_specs=[VMEM] * 3, out_specs=[VMEM] * 5, name="prepare"
    )(left, right, eigen)


def halves(v):
    return v[:, :FB] + v[:, FB:]


def beside(v):
    return jnp.concatenate([v[:WIDE], v[WIDE:]], axis=1)


def precondition(x, out, lt, l, rr, rrt, inv):
    def group(g, carry):
        spots = [
            [pl.ds(pl.multiple_of((g * PAIRS + q) * 32 + 16 * k, 16), 16) for k in range(2)]
            for q in range(PAIRS)
        ]
        values = []
        for two in spots:
            z = jnp.concatenate(
                [
                    jnp.concatenate([x[at, a * FB : (a + 1) * FB] for a in range(FA)], axis=0)
                    for at in two
                ],
                axis=1,
            )
            v = dot(lt[0], z) + dot(lt[1], z)
            values.append(jnp.concatenate([v[:, :FB], v[:, FB:]], axis=0))
        values = [halves(dot(jnp.concatenate(split(v), axis=1), rr[...])) for v in values]
        scale = jnp.concatenate([inv[...], inv[...]], axis=0)
        values = [v * scale for v in values]
        values = [halves(dot(jnp.concatenate(split(v), axis=1), rrt[...])) for v in values]
        for two, v in zip(spots, values):
            high, low = [beside(part) for part in split(v)]
            v = (dot(l[0], high) + dot(l[1], high) + dot(l[0], low)).astype(bf16)
            for k, at in enumerate(two):
                for a in range(FA):
                    out[at, a * FB : (a + 1) * FB] = v[
                        a * 16 : (a + 1) * 16, k * FB : (k + 1) * FB
                    ]
        return carry

    lax.fori_loop(0, x.shape[0] // (32 * PAIRS), group, 0)


def whole(a):
    return pl.BlockSpec(a.shape, lambda *_: (0,) * len(a.shape))


def own_kernel(lower, x, lt, l, rr, rrt, inv, out):
    @pl.when(lower[0] == 1)
    def _():
        precondition(x, out, lt, l, rr, rrt, inv)

    @pl.when(lower[0] == 0)
    def _():
        out[...] = x[...]


def own_side(lower, x, ready):
    rows = pl.BlockSpec((128, COLS), lambda i: (i, 0))
    return pl.pallas_call(
        own_kernel,
        grid=(ROWS // 128,),
        out_shape=jax.ShapeDtypeStruct(x.shape, bf16),
        in_specs=[SMEM, rows] + [whole(a) for a in ready],
        out_specs=rows,
        name="own",
        **params(5 << 30, 4 << 20),
    )(lower, x, *ready)


def piece_kernel(at, n, half, lower, x, *rest):
    out, sems = rest[-2:]
    columns = pl.ds(pl.multiple_of(lower[0] * (COLS // 2), COLS // 2), COLS // 2)
    copies = []
    for i in range(8):
        rows = pl.ds(((i % 2) * 4 + i // 2) * SHARE + at, n)
        source = x.at[rows, columns] if half else x.at[rows]
        copies.append(pltpu.make_async_copy(source, out.at[pl.ds(i * n, n)], sems.at[i]))
    for copy in copies:
        copy.start()
    for copy in copies:
        copy.wait()


def piece(lower, x, at, n, half, after=None):
    after = [] if after is None else [after]
    columns = COLS // 2 if half else COLS
    return pl.pallas_call(
        functools.partial(piece_kernel, at, n, half),
        out_shape=jax.ShapeDtypeStruct((8 * n, columns), bf16),
        in_specs=[SMEM, ANY] + [ANY] * len(after),
        out_specs=ANY,
        scratch_shapes=[pltpu.SemaphoreType.DMA((8,))],
        name="piece",
        **params(0, 2 * 8 * n * columns * 2),
    )(lower, x, *after)


def tile_kernel(raw, lower, y, own, *rest):
    if not raw:
        out = rest[-1]
        out[...] = dot_t(y[...], own[...]) * SCALE
        return
    ready, out, held = rest[:5], rest[-2], rest[-1]

    @pl.when(lower[0] == 1)
    def _():
        out[...] = dot_t(y[...], own[...]) * SCALE

    @pl.when(lower[0] == 0)
    def _():
        precondition(y, held, *ready)
        out[...] = dot_t(held[...], own[...]) * SCALE


def tile(raw, lower, y, own, ready, after=None):
    after = [] if after is None else [after]
    ready = ready if raw else ()
    out = pl.pallas_call(
        functools.partial(tile_kernel, raw),
        out_shape=jax.ShapeDtypeStruct((y.shape[0], ROWS), f32),
        in_specs=[SMEM, VMEM, VMEM] + [VMEM] * len(ready) + [ANY] * len(after),
        out_specs=VMEM,
        scratch_shapes=[pltpu.VMEM(y.shape, bf16)] if raw else [],
        name="tile",
        **params(2 * y.shape[0] * ROWS * COLS, 3 << 20),
    )(lower, y, own, *ready, *after)
    return out.reshape(4, 2, y.shape[0] // 8, ROWS)


def fold_kernel(z_hi, parts, keep, send):
    z = z_hi[0]
    keep[...] = parts[0, z] + parts[1, z] + parts[2, z] + parts[3, z]
    o = 1 - z
    send[...] = parts[0, o] + parts[1, o] + parts[2, o] + parts[3, o]


def fold(z_hi, parts):
    shape = jax.ShapeDtypeStruct(parts.shape[2:], f32)
    return pl.pallas_call(
        fold_kernel,
        out_shape=(shape, shape),
        in_specs=[SMEM, VMEM],
        out_specs=(VMEM, VMEM),
        name="fold",
        **params(0, 4 * parts.size),
    )(z_hi, parts)


def summed(z_hi, parts):
    parts = lax.all_to_all(parts, "feat", 0, 0, axis_index_groups=Y_GROUPS)
    keep, send = fold(z_hi, parts)
    return keep, lax.ppermute(send, "feat", [(f, f ^ 4) for f in range(8)])


def swap(level, x):
    return lax.ppermute(x, "blk", [(b, b ^ (1 << level)) for b in range(64)])


def join_kernel(*refs):
    out, at = refs[-1], 0
    for a, b in zip(refs[:-1:2], refs[1:-1:2]):
        out[at : at + a.shape[0]] = a[...] + b[...]
        at += a.shape[0]


def join(pieces):
    flat = [a for both in pieces for a in both]
    return pl.pallas_call(
        join_kernel,
        out_shape=jax.ShapeDtypeStruct((SHARE, ROWS), f32),
        in_specs=[VMEM] * len(flat),
        out_specs=VMEM,
        name="join",
        **params(0, 4 * SHARE * ROWS * 3),
    )(*flat)


def by_pieces(sizes, level, x, ready, lower, z_hi):
    own = own_side(lower, x, ready)
    done, at, arrived = [], 0, None
    for k, n in enumerate(sizes):
        arrived = swap(level, piece(lower, x if k == 0 else own, at, n, False, arrived))
        done.append(summed(z_hi, tile(k == 0, lower, arrived, own, ready)))
        at += n
    return join(done)


def half_kernel(n, lower, y, own, *rest):
    out = rest[-1]

    def both(mine):
        rows = dot_t(y[...], mine) * SCALE
        across = dot_t(mine, y[...]) * SCALE
        for i in range(8):
            out[i, :n] = rows[i * n : (i + 1) * n]
            first = ((i % 2) * 4 + i // 2) * SHARE
            for q in range(SHARE // n):
                out[i, n:, q * 8 * n : (q + 1) * 8 * n] = across[
                    first + q * n : first + (q + 1) * n
                ]

    @pl.when(lower[0] == 1)
    def _():
        both(own[:, : COLS // 2])

    @pl.when(lower[0] == 0)
    def _():
        both(own[:, COLS // 2 :])


def half_tile(n, lower, y, own, after=None):
    after = [] if after is None else [after]
    out = pl.pallas_call(
        functools.partial(half_kernel, n),
        out_shape=jax.ShapeDtypeStruct((8, 2 * n, ROWS), f32),
        in_specs=[SMEM, VMEM, VMEM] + [ANY] * len(after),
        out_specs=VMEM,
        name="half_tile",
        **params(4 * y.shape[0] * ROWS * COLS // 2, 3 << 20),
    )(lower, y, own, *after)
    return out.reshape(4, 2, 2 * n, ROWS)


def last_kernel(n, *refs):
    out, count = refs[-1], SHARE // n
    blocks = []
    for c in range(count):
        far = refs[3 * c + 2][...]
        blocks.append(
            jnp.concatenate([far[:, q * 8 * n : (q + 1) * 8 * n] for q in range(SHARE // n)], axis=0)
        )
    spread = []
    for f in range(8):
        i = (f % 4) * 2 + f // 4
        spread += [block[:, i * n : (i + 1) * n] for block in blocks]
    out[...] = jnp.concatenate(spread, axis=1)
    for c in range(count):
        out[c * n : (c + 1) * n] += refs[3 * c][:n] + refs[3 * c + 1][:n]


def last(n, pieces):
    flat = [a for three in pieces for a in three]
    return pl.pallas_call(
        functools.partial(last_kernel, n),
        out_shape=jax.ShapeDtypeStruct((SHARE, ROWS), f32),
        in_specs=[VMEM] * len(flat),
        out_specs=VMEM,
        name="last",
        **params(0, 4 * SHARE * ROWS * 6),
    )(*flat)


def by_halves(n, level, x, ready, lower, z_hi):
    own = own_side(lower, x, ready)
    done, arrived, kept = [], None, None
    for c in range(SHARE // n):
        arrived = swap(level, piece(lower, own, c * n, n, True, arrived))
        kept, got = summed(z_hi, half_tile(n, lower, arrived, own, kept))
        done.append((kept, got, swap(level, kept[n:] + got[n:])))
    return last(n, done)


PLANS = [
    functools.partial(by_pieces, (32, 32), 0),
    functools.partial(by_halves, 32, 1),
    functools.partial(by_halves, 32, 2),
    functools.partial(by_halves, 32, 3),
    functools.partial(by_halves, 16, 4),
    functools.partial(by_halves, 16, 5),
]


def body(grads, basis_left, basis_right, eigen, partner):
    mask = partner[0, 0]
    lower = (jnp.bitwise_and(lax.axis_index("blk"), mask) == 0).astype(jnp.int32).reshape(1)
    z_hi = (lax.axis_index("feat") // 4).astype(jnp.int32).reshape(1)
    level = sum((mask >= 1 << k).astype(jnp.int32) for k in range(1, 6))
    ready = prepared(basis_left[0], basis_right[0], eigen.reshape(FA, FB))
    out = lax.switch(level, PLANS, grads, ready, lower, z_hi)
    return out.T[None]


def solution(mesh):
    placed = (P("blk", "feat"), P("feat", None, None), P("feat", None, None), P("feat"), P())
    return jax.shard_map(
        body, mesh=mesh, in_specs=placed, out_specs=P(None, "blk", "feat"), check_vma=False
    )
```

```python
import functools

import jax
import jax.numpy as jnp
from jax import lax
from jax.experimental import pallas as pl
from jax.experimental.pallas import tpu as pltpu
from jax.sharding import PartitionSpec as P

FA = 16
FB = 128
ROWS = 512
COLS = FA * FB
WIDE = 16 * FA
SHARE = 64
PAIRS = 4
SCALE = 1.0 / 128.0
Y_GROUPS = [[0, 1, 2, 3], [4, 5, 6, 7]]
VMEM = pl.BlockSpec(memory_space=pltpu.VMEM)
SMEM = pl.BlockSpec(memory_space=pltpu.SMEM)
ANY = pl.BlockSpec(memory_space=pl.ANY)
f32, bf16 = jnp.float32, jnp.bfloat16


def params(flops, moved):
    return dict(
        compiler_params=pltpu.CompilerParams(vmem_limit_bytes=28 << 20),
        cost_estimate=pl.CostEstimate(flops=flops, bytes_accessed=moved, transcendentals=0),
    )


def split(v):
    high = v.astype(bf16)
    return high, (v - high.astype(f32)).astype(bf16)


def dot(a, b):
    return jnp.dot(a, b, preferred_element_type=f32)


def dot_t(a, b):
    return lax.dot_general(a, b, (((1,), (1,)), ((), ())), preferred_element_type=f32)


def prepare(left, right, eigen, lt, l, rr, rrt, inv):
    spread = (
        lax.broadcasted_iota(jnp.int32, (WIDE, FA), 0) >> 4
        == lax.broadcasted_iota(jnp.int32, (WIDE, FA), 1)
    ).astype(bf16)
    same = (lax.broadcasted_iota(jnp.int32, (WIDE, WIDE), 0) & 15) == (
        lax.broadcasted_iota(jnp.int32, (WIDE, WIDE), 1) & 15
    )
    for k, v in enumerate(split(left[...])):
        wide = dot_t(dot(spread, v).astype(bf16), spread)
        l[k] = jnp.where(same, wide, 0.0).astype(bf16)
        wide = dot_t(dot_t(spread, v).astype(bf16), spread)
        lt[k] = jnp.where(same, wide, 0.0).astype(bf16)
    for out, basis in ((rr, right[...]), (rrt, right[...].T)):
        for k, v in enumerate(split(basis)):
            out[:FB, k * FB : (k + 1) * FB] = v
            out[FB:, k * FB : (k + 1) * FB] = v
    reciprocal = 1.0 / (eigen[...] + 0.1)
    inv[...] = jnp.broadcast_to(reciprocal[:, None, :], (FA, 16, FB)).reshape(WIDE, FB)


PREPARED = (
    jax.ShapeDtypeStruct((2, WIDE, WIDE), bf16),
    jax.ShapeDtypeStruct((2, WIDE, WIDE), bf16),
    jax.ShapeDtypeStruct((2 * FB, 2 * FB), bf16),
    jax.ShapeDtypeStruct((2 * FB, 2 * FB), bf16),
    jax.ShapeDtypeStruct((WIDE, FB), f32),
)


def prepared(left, right, eigen):
    return pl.pallas_call(
        prepare, out_shape=PREPARED, in_specs=[VMEM] * 3, out_specs=[VMEM] * 5, name="prepare"
    )(left, right, eigen)


def halves(v):
    return v[:, :FB] + v[:, FB:]


def beside(v):
    return jnp.concatenate([v[:WIDE], v[WIDE:]], axis=1)


def precondition(groups, load, store, lt, l, rr, rrt, inv):
    def some(g, carry):
        pairs = [[(g * PAIRS + q) * 2 + k for k in range(2)] for q in range(PAIRS)]
        values = []
        for two in pairs:
            z = jnp.concatenate(
                [jnp.concatenate([load(t, a) for a in range(FA)], axis=0) for t in two], axis=1
            )
            v = dot(lt[0], z) + dot(lt[1], z)
            values.append(jnp.concatenate([v[:, :FB], v[:, FB:]], axis=0))
        values = [halves(dot(jnp.concatenate(split(v), axis=1), rr[...])) for v in values]
        scale = jnp.concatenate([inv[...], inv[...]], axis=0)
        values = [v * scale for v in values]
        values = [halves(dot(jnp.concatenate(split(v), axis=1), rrt[...])) for v in values]
        for two, v in zip(pairs, values):
            high, low = [beside(part) for part in split(v)]
            v = (dot(l[0], high) + dot(l[1], high) + dot(l[0], low)).astype(bf16)
            for k, t in enumerate(two):
                for a in range(FA):
                    store(t, a, v[a * 16 : (a + 1) * 16, k * FB : (k + 1) * FB])
        return carry

    lax.fori_loop(0, groups // (2 * PAIRS), some, 0)


def columns_of(a):
    return slice(a * FB, (a + 1) * FB)


def rows_of(t):
    return pl.ds(pl.multiple_of(t * 16, 16), 16)


def precondition_rows(x, out, *ready):
    def store(t, a, v):
        out[rows_of(t), columns_of(a)] = v

    precondition(x.shape[0] // 16, lambda t, a: x[rows_of(t), columns_of(a)], store, *ready)


def whole(a):
    return pl.BlockSpec(a.shape, lambda *_: (0,) * len(a.shape))


def own_kernel(lower, x, lt, l, rr, rrt, inv, out):
    @pl.when(lower[0] == 1)
    def _():
        precondition_rows(x, out, lt, l, rr, rrt, inv)

    @pl.when(lower[0] == 0)
    def _():
        out[...] = x[...]


def own_side(lower, x, ready):
    rows = pl.BlockSpec((128, COLS), lambda i: (i, 0))
    return pl.pallas_call(
        own_kernel,
        grid=(ROWS // 128,),
        out_shape=jax.ShapeDtypeStruct(x.shape, bf16),
        in_specs=[SMEM, rows] + [whole(a) for a in ready],
        out_specs=rows,
        name="own",
        **params(5 << 30, 4 << 20),
    )(lower, x, *ready)


def share_of(i):
    return (i % 2) * 4 + i // 2


def piece_kernel(at, n, x, out, sems):
    copies = [
        pltpu.make_async_copy(
            x.at[pl.ds(share_of(i) * SHARE + at, n)], out.at[pl.ds(i * n, n)], sems.at[i]
        )
        for i in range(8)
    ]
    for copy in copies:
        copy.start()
    for copy in copies:
        copy.wait()


def piece(x, at, n):
    return pl.pallas_call(
        functools.partial(piece_kernel, at, n),
        out_shape=jax.ShapeDtypeStruct((8 * n, COLS), bf16),
        in_specs=[ANY],
        out_specs=ANY,
        scratch_shapes=[pltpu.SemaphoreType.DMA((8,))],
        name="piece",
        **params(0, 2 * 8 * n * COLS * 2),
    )(x)


def later_kernel(x, after, out, sem):
    copy = pltpu.make_async_copy(x, out, sem)
    copy.start()
    copy.wait()


def later(x, after):
    return pl.pallas_call(
        later_kernel,
        out_shape=jax.ShapeDtypeStruct(x.shape, x.dtype),
        in_specs=[ANY, ANY],
        out_specs=ANY,
        scratch_shapes=[pltpu.SemaphoreType.DMA],
        name="later",
        **params(0, 4 * x.size),
    )(x, after)


def tile_kernel(raw, lower, y, own, *rest):
    if not raw:
        out = rest[-1]
        out[...] = dot_t(y[...], own[...]) * SCALE
        return
    ready, out, held = rest[:5], rest[-2], rest[-1]

    @pl.when(lower[0] == 1)
    def _():
        out[...] = dot_t(y[...], own[...]) * SCALE

    @pl.when(lower[0] == 0)
    def _():
        precondition_rows(y, held, *ready)
        out[...] = dot_t(held[...], own[...]) * SCALE


def tile(raw, lower, y, own, ready, after=None):
    after = [] if after is None else [after]
    ready = ready if raw else ()
    out = pl.pallas_call(
        functools.partial(tile_kernel, raw),
        out_shape=jax.ShapeDtypeStruct((y.shape[0], ROWS), f32),
        in_specs=[SMEM, VMEM, VMEM] + [VMEM] * len(ready) + [ANY] * len(after),
        out_specs=VMEM,
        scratch_shapes=[pltpu.VMEM(y.shape, bf16)] if raw else [],
        name="tile",
        **params(2 * y.shape[0] * ROWS * COLS, 3 << 20),
    )(lower, y, own, *ready, *after)
    return out.reshape(4, 2, y.shape[0] // 8, ROWS)


def fold_kernel(count, parts, *rest):
    at = 0
    for out in rest[-count:]:
        rows = slice(at, at + out.shape[1])
        for z in range(2):
            four = [parts[y, z, rows].astype(f32) for y in range(4)]
            out[z] = (four[0] + four[1]) + (four[2] + four[3])
        at += out.shape[1]


def fold(parts, count, after=()):
    _, _, rows, columns = parts.shape
    shape = jax.ShapeDtypeStruct((2, rows // count, columns), f32)
    return pl.pallas_call(
        functools.partial(fold_kernel, count),
        out_shape=(shape,) * count,
        in_specs=[VMEM] + [ANY] * len(after),
        out_specs=(VMEM,) * count,
        name="fold",
        **params(0, 5 * parts.size),
    )(parts, *after)


def over_y(parts):
    return lax.all_to_all(parts, "feat", 0, 0, axis_index_groups=Y_GROUPS)


def over_z(x):
    return lax.ppermute(x, "feat", [(f, f ^ 4) for f in range(8)])


def swap(level, x):
    return lax.ppermute(x, "blk", [(b, b ^ (1 << level)) for b in range(64)])


def join_kernel(z_hi, *refs):
    sums, outs = refs[:-2], refs[-2:]
    for z, out in zip((z_hi[0], 1 - z_hi[0]), outs):
        at = 0
        for part in sums:
            out[at : at + part.shape[1]] = part[z].astype(out.dtype)
            at += part.shape[1]


def merge_kernel(n, z_hi, *refs):
    outs, count = refs[-2:], SHARE // n
    for z, out in zip((z_hi[0], 1 - z_hi[0]), outs):
        near = jnp.concatenate([refs[2 * c][z] for c in range(count)], axis=0)
        far = [refs[2 * c + 1][z] for c in range(count)]
        far = [
            jnp.concatenate([v[:, q * 8 * n : (q + 1) * 8 * n] for q in range(count)], axis=0)
            for v in far
        ]
        v = near + jnp.concatenate(far, axis=1)
        out[...] = jnp.concatenate(
            [
                v[:, (c * 8 + (f % 4) * 2 + f // 4) * n :][:, :n]
                for f in range(8)
                for c in range(count)
            ],
            axis=1,
        ).astype(out.dtype)


def finish(kernel, z_hi, sums):
    shape = jax.ShapeDtypeStruct((SHARE, ROWS), f32)
    return pl.pallas_call(
        kernel,
        out_shape=(shape, jax.ShapeDtypeStruct((SHARE, ROWS), bf16)),
        in_specs=[SMEM] + [VMEM] * len(sums),
        out_specs=(VMEM, VMEM),
        name="finish",
        **params(0, 4 * SHARE * ROWS * 6),
    )(z_hi, *sums)


def by_pieces(sizes, level, x, ready, lower, z_hi):
    own = own_side(lower, x, ready)
    sums, at, arrived = [], 0, None
    for k, n in enumerate(sizes):
        leaving = piece(x if k == 0 else own, at, n)
        arrived = swap(level, leaving if k == 0 else later(leaving, arrived))
        sums += fold(over_y(tile(k == 0, lower, arrived, own, ready)), 1)
        at += n
    return finish(join_kernel, z_hi, sums)


def first_kernel(n, lower, x, *rest):
    ready, (out, leaving) = rest[:5], rest[5:]
    per = n // 16

    def place(t):
        share, row = share_of(t // per), pl.multiple_of((t % per) * 16, 16)
        return share, pl.ds(row, 16)

    def load(t, a):
        share, rows = place(t)
        return x[share, rows, columns_of(a)]

    def store(t, a, v):
        out[rows_of(t), columns_of(a)] = v
        if a >= FA // 2:
            leaving[rows_of(t), columns_of(a - FA // 2)] = v

    @pl.when(lower[0] == 1)
    def _():
        precondition(8 * per, load, store, *ready)

    @pl.when(lower[0] == 0)
    def _():
        for i in range(8):
            out[i * n : (i + 1) * n] = x[share_of(i)]
            leaving[i * n : (i + 1) * n] = x[share_of(i), :, : COLS // 2]


def first(c, n, lower, x, ready):
    return pl.pallas_call(
        functools.partial(first_kernel, n),
        grid=(1,),
        out_shape=(
            jax.ShapeDtypeStruct((8 * n, COLS), bf16),
            jax.ShapeDtypeStruct((8 * n, COLS // 2), bf16),
        ),
        in_specs=[SMEM, pl.BlockSpec((8, n, COLS), lambda i: (0, c, 0))]
        + [whole(a) for a in ready],
        out_specs=(
            pl.BlockSpec((8 * n, COLS), lambda i: (0, 0)),
            pl.BlockSpec((8 * n, COLS // 2), lambda i: (0, 0)),
        ),
        name="first",
        **params(2 << 30, 4 << 20),
    )(lower, x.reshape(8, SHARE, COLS), *ready)


def half_kernel(n, lower, y, *rest):
    out, count = rest[-1], SHARE // n

    def both(columns):
        for c in range(count):
            mine, at = rest[c][:, columns], slice(c * 8 * n, (c + 1) * 8 * n)
            rows = (dot_t(y[...], mine) * SCALE).astype(out.dtype)
            across = (dot_t(mine, y[...]) * SCALE).astype(out.dtype)
            for i in range(8):
                out[i, :n, at] = rows[i * n : (i + 1) * n]
                out[i, n:, at] = across[i * n : (i + 1) * n]

    @pl.when(lower[0] == 1)
    def _():
        both(slice(0, COLS // 2))

    @pl.when(lower[0] == 0)
    def _():
        both(slice(COLS // 2, COLS))


def half_tile(n, lower, y, owns, after):
    out = pl.pallas_call(
        functools.partial(half_kernel, n),
        out_shape=jax.ShapeDtypeStruct((8, 2 * n, ROWS), bf16),
        in_specs=[SMEM, VMEM] + [VMEM] * len(owns) + [ANY] * len(after),
        out_specs=VMEM,
        name="half_tile",
        **params(4 * y.shape[0] * ROWS * COLS // 2, 3 << 20),
    )(lower, y, *owns, *after)
    return out.reshape(4, 2, 2 * n, ROWS)


def by_halves(n, level, x, ready, lower, z_hi):
    count = SHARE // n
    pairs = [first(c, n, lower, x, ready) for c in range(count)]
    owns = [own for own, _ in pairs]
    arrived = swap(level, pairs[0][1])
    sums, near, after = [], (), ()
    for c in range(count):
        here, order = arrived, near
        if c + 1 < count:
            leaving = later(pairs[c + 1][1], here)
            arrived = swap(level, leaving)
            order = (*order, leaving)
        part, far = fold(over_y(half_tile(n, lower, here, owns, order)), 2, after)
        near, after = (part,), (swap(level, far),)
        sums += [part, *after]
    return finish(functools.partial(merge_kernel, n), z_hi, sums)


PLANS = [functools.partial(by_pieces, (32, 32), 0)]
PLANS += [functools.partial(by_halves, 32, k) for k in range(1, 6)]


def body(grads, basis_left, basis_right, eigen, partner):
    mask = partner[0, 0]
    lower = (jnp.bitwise_and(lax.axis_index("blk"), mask) == 0).astype(jnp.int32).reshape(1)
    z_hi = (lax.axis_index("feat") // 4).astype(jnp.int32).reshape(1)
    level = sum((mask >= 1 << k).astype(jnp.int32) for k in range(1, 6))
    ready = prepared(basis_left[0], basis_right[0], eigen.reshape(FA, FB))
    keep, send = lax.switch(level, PLANS, grads, ready, lower, z_hi)
    return (keep + over_z(send)).T[None]


def solution(mesh):
    placed = (P("blk", "feat"), P("feat", None, None), P("feat", None, None), P("feat"), P())
    return jax.shard_map(
        body, mesh=mesh, in_specs=placed, out_specs=P(None, "blk", "feat"), check_vma=False
    )
```

```python
import functools

import jax
import jax.numpy as jnp
from jax import lax
from jax.experimental import pallas as pl
from jax.experimental.pallas import tpu as pltpu
from jax.sharding import PartitionSpec as P

FA = 16
FB = 128
ROWS = 512
COLS = FA * FB
WIDE = 16 * FA
SHARE = 64
PAIRS = 4
HALF = COLS // 2
SCALE = 1.0 / 128.0
Y_GROUPS = [[0, 1, 2, 3], [4, 5, 6, 7]]
VMEM = pl.BlockSpec(memory_space=pltpu.VMEM)
SMEM = pl.BlockSpec(memory_space=pltpu.SMEM)
f32, bf16 = jnp.float32, jnp.bfloat16


def params(flops, moved, grant=28):
    return dict(
        compiler_params=pltpu.CompilerParams(vmem_limit_bytes=grant << 20),
        cost_estimate=pl.CostEstimate(flops=flops, bytes_accessed=moved, transcendentals=0),
    )


def split(v):
    high = v.astype(bf16)
    return high, (v - high.astype(f32)).astype(bf16)


def dot(a, b):
    return jnp.dot(a, b, preferred_element_type=f32)


def dot_t(a, b):
    return lax.dot_general(a, b, (((1,), (1,)), ((), ())), preferred_element_type=f32)


def prepare(left, right, eigen, lt, l, rr, rrt, inv):
    spread = (
        lax.broadcasted_iota(jnp.int32, (WIDE, FA), 0) >> 4
        == lax.broadcasted_iota(jnp.int32, (WIDE, FA), 1)
    ).astype(bf16)
    same = (lax.broadcasted_iota(jnp.int32, (WIDE, WIDE), 0) & 15) == (
        lax.broadcasted_iota(jnp.int32, (WIDE, WIDE), 1) & 15
    )
    for k, v in enumerate(split(left[...])):
        wide = dot_t(dot(spread, v).astype(bf16), spread)
        l[k] = jnp.where(same, wide, 0.0).astype(bf16)
        wide = dot_t(dot_t(spread, v).astype(bf16), spread)
        lt[k] = jnp.where(same, wide, 0.0).astype(bf16)
    for out, basis in ((rr, right[...]), (rrt, right[...].T)):
        for k, v in enumerate(split(basis)):
            out[:FB, k * FB : (k + 1) * FB] = v
            out[FB:, k * FB : (k + 1) * FB] = v
    reciprocal = 1.0 / (eigen[...] + 0.1)
    inv[...] = jnp.broadcast_to(reciprocal[:, None, :], (FA, 16, FB)).reshape(WIDE, FB)


PREPARED = (
    pltpu.VMEM((2, WIDE, WIDE), bf16),
    pltpu.VMEM((2, WIDE, WIDE), bf16),
    pltpu.VMEM((2 * FB, 2 * FB), bf16),
    pltpu.VMEM((2 * FB, 2 * FB), bf16),
    pltpu.VMEM((WIDE, FB), f32),
)


def halves(v):
    return v[:, :FB] + v[:, FB:]


def beside(v):
    return jnp.concatenate([v[:WIDE], v[WIDE:]], axis=1)


def precondition(x, store, lt, l, rr, rrt, inv):
    def some(g, carry):
        pairs = [
            [pl.ds(pl.multiple_of(((g * PAIRS + q) * 2 + k) * 16, 16), 16) for k in range(2)]
            for q in range(PAIRS)
        ]
        values = []
        for two in pairs:
            z = jnp.concatenate(
                [
                    jnp.concatenate([x[at, a * FB : (a + 1) * FB] for a in range(FA)], axis=0)
                    for at in two
                ],
                axis=1,
            )
            v = dot(lt[0], z) + dot(lt[1], z)
            values.append(jnp.concatenate([v[:, :FB], v[:, FB:]], axis=0))
        values = [halves(dot(jnp.concatenate(split(v), axis=1), rr[...])) for v in values]
        scale = jnp.concatenate([inv[...], inv[...]], axis=0)
        values = [v * scale for v in values]
        values = [halves(dot(jnp.concatenate(split(v), axis=1), rrt[...])) for v in values]
        for two, v in zip(pairs, values):
            high, low = [beside(part) for part in split(v)]
            v = (dot(l[0], high) + dot(l[1], high) + dot(l[0], low)).astype(bf16)
            for k, at in enumerate(two):
                for a in range(FA):
                    store(at, a, v[a * 16 : (a + 1) * 16, k * FB : (k + 1) * FB])
        return carry

    lax.fori_loop(0, x.shape[0] // (32 * PAIRS), some, 0)


def whole(a):
    return pl.BlockSpec(a.shape, lambda *_: (0,) * len(a.shape))


def own_kernel(me, partner, x, left, right, eigen, stays, leaves, *ready):
    lower = jnp.bitwise_and(me[0], partner[0, 0]) == 0

    @pl.when(lower)
    def _():
        @pl.when(pl.program_id(0) == 0)
        def _():
            prepare(left, right, eigen, *ready)

        def store(at, a, v):
            out, a = (stays, a) if a < FA // 2 else (leaves, a - FA // 2)
            out[at, a * FB : (a + 1) * FB] = v

        precondition(x, store, *ready)

    @pl.when(jnp.logical_not(lower))
    def _():
        stays[...] = x[:, HALF:]
        leaves[...] = x[:, :HALF]


def own_side(me, partner, x, left, right, eigen):
    step = 32 * PAIRS
    rows = pl.BlockSpec((step, HALF), lambda i: (i, 0))
    shape = jax.ShapeDtypeStruct((ROWS, HALF), bf16)
    return pl.pallas_call(
        own_kernel,
        grid=(ROWS // step,),
        out_shape=(shape, shape),
        in_specs=[SMEM, SMEM, pl.BlockSpec((step, COLS), lambda i: (i, 0))]
        + [whole(a) for a in (left, right, eigen)],
        out_specs=(rows, rows),
        scratch_shapes=PREPARED,
        name="own",
        **params(5 << 30, 4 << 20, 56),
    )(me, partner, x, left, right, eigen)


def tile_kernel(a, b, out):
    v = (dot_t(a[...], b[...]) * SCALE).astype(out.dtype)
    for i in range(8):
        first = ((i % 2) * 4 + i // 2) * SHARE
        out[i] = v[first : first + SHARE]


def tile(a, b):
    out = pl.pallas_call(
        tile_kernel,
        out_shape=jax.ShapeDtypeStruct((8, SHARE, ROWS), bf16),
        in_specs=[VMEM, VMEM],
        out_specs=VMEM,
        name="tile",
        **params(2 * ROWS * ROWS * HALF, 3 << 20),
    )(a, b)
    return out.reshape(4, 2, SHARE, ROWS)


def fold_kernel(parts, out):
    for z in range(2):
        four = [parts[y, z].astype(f32) for y in range(4)]
        out[z] = (four[0] + four[1]) + (four[2] + four[3])


def over_y(tile):
    parts = lax.all_to_all(tile, "feat", 0, 0, axis_index_groups=Y_GROUPS)
    return pl.pallas_call(
        fold_kernel,
        out_shape=jax.ShapeDtypeStruct((2, SHARE, ROWS), f32),
        in_specs=[VMEM],
        out_specs=VMEM,
        name="fold",
        **params(0, 4 * parts.size),
    )(parts)


def merge_kernel(z_hi, near, far, keep, send):
    z = z_hi[0]
    keep[...] = near[z] + far[z]
    send[...] = (near[1 - z] + far[1 - z]).astype(send.dtype)


def merge(z_hi, near, far):
    shape = (SHARE, ROWS)
    return pl.pallas_call(
        merge_kernel,
        out_shape=(jax.ShapeDtypeStruct(shape, f32), jax.ShapeDtypeStruct(shape, bf16)),
        in_specs=[SMEM, VMEM, VMEM],
        out_specs=(VMEM, VMEM),
        name="merge",
        **params(0, 4 * SHARE * ROWS * 6),
    )(z_hi, near, far)


def over_z(x):
    return lax.ppermute(x, "feat", [(f, f ^ 4) for f in range(8)])


def swap(level, x):
    def at(k):
        return lambda v: lax.ppermute(v, "blk", [(b, b ^ (1 << k)) for b in range(64)])

    return lax.switch(level, [at(k) for k in range(6)], x)


def body(grads, basis_left, basis_right, eigen, partner):
    mask = partner[0, 0]
    blk = lax.axis_index("blk").astype(jnp.int32).reshape(1)
    z_hi = (lax.axis_index("feat") // 4).astype(jnp.int32).reshape(1)
    level = sum((mask >= 1 << k).astype(jnp.int32) for k in range(1, 6))
    stays, leaves = own_side(
        blk, partner, grads, basis_left[0], basis_right[0], eigen.reshape(FA, FB)
    )
    arrived = swap(level, leaves)
    far = over_y(tile(stays, arrived))
    near = over_y(tile(arrived, stays))
    keep, send = merge(z_hi, near, swap(level, far))
    return (keep + over_z(send)).T[None]


def solution(mesh):
    placed = (P("blk", "feat"), P("feat", None, None), P("feat", None, None), P("feat"), P())
    return jax.shard_map(
        body, mesh=mesh, in_specs=placed, out_specs=P(None, "blk", "feat"), check_vma=False
    )
```

```python
import functools

import jax
import jax.numpy as jnp
from jax import lax
from jax.experimental import pallas as pl
from jax.experimental.pallas import tpu as pltpu
from jax.sharding import PartitionSpec as P

FA = 16
FB = 128
ROWS = 512
COLS = FA * FB
WIDE = 16 * FA
SHARE = 64
PAIRS = 4
HALF = COLS // 2
SCALE = 1.0 / 128.0
Y_GROUPS = [[0, 1, 2, 3], [4, 5, 6, 7]]
VMEM = pl.BlockSpec(memory_space=pltpu.VMEM)
SMEM = pl.BlockSpec(memory_space=pltpu.SMEM)
f32, bf16 = jnp.float32, jnp.bfloat16


def params(flops, moved, grant=28):
    return dict(
        compiler_params=pltpu.CompilerParams(vmem_limit_bytes=grant << 20),
        cost_estimate=pl.CostEstimate(flops=flops, bytes_accessed=moved, transcendentals=0),
    )


def split(v):
    high = v.astype(bf16)
    return high, (v - high.astype(f32)).astype(bf16)


def dot(a, b):
    return jnp.dot(a, b, preferred_element_type=f32)


def dot_t(a, b):
    return lax.dot_general(a, b, (((1,), (1,)), ((), ())), preferred_element_type=f32)


def prepare(left, right, eigen, lt, l, rr, rrt, inv):
    spread = (
        lax.broadcasted_iota(jnp.int32, (WIDE, FA), 0) >> 4
        == lax.broadcasted_iota(jnp.int32, (WIDE, FA), 1)
    ).astype(bf16)
    same = (lax.broadcasted_iota(jnp.int32, (WIDE, WIDE), 0) & 15) == (
        lax.broadcasted_iota(jnp.int32, (WIDE, WIDE), 1) & 15
    )
    for k, v in enumerate(split(left[...])):
        wide = dot_t(dot(spread, v).astype(bf16), spread)
        l[k] = jnp.where(same, wide, 0.0).astype(bf16)
        wide = dot_t(dot_t(spread, v).astype(bf16), spread)
        lt[k] = jnp.where(same, wide, 0.0).astype(bf16)
    for out, basis in ((rr, right[...]), (rrt, right[...].T)):
        for k, v in enumerate(split(basis)):
            out[:FB, k * FB : (k + 1) * FB] = v
            out[FB:, k * FB : (k + 1) * FB] = v
    reciprocal = 1.0 / (eigen[...] + 0.1)
    inv[...] = jnp.broadcast_to(reciprocal[:, None, :], (FA, 16, FB)).reshape(WIDE, FB)


PREPARED = (
    pltpu.VMEM((2, WIDE, WIDE), bf16),
    pltpu.VMEM((2, WIDE, WIDE), bf16),
    pltpu.VMEM((2 * FB, 2 * FB), bf16),
    pltpu.VMEM((2 * FB, 2 * FB), bf16),
    pltpu.VMEM((WIDE, FB), f32),
)


def halves(v):
    return v[:, :FB] + v[:, FB:]


def beside(v):
    return jnp.concatenate([v[:WIDE], v[WIDE:]], axis=1)


def precondition(x, store, lt, l, rr, rrt, inv):
    def some(g, carry):
        pairs = [
            [pl.ds(pl.multiple_of(((g * PAIRS + q) * 2 + k) * 16, 16), 16) for k in range(2)]
            for q in range(PAIRS)
        ]
        values = []
        for two in pairs:
            z = jnp.concatenate(
                [
                    jnp.concatenate([x[at, a * FB : (a + 1) * FB] for a in range(FA)], axis=0)
                    for at in two
                ],
                axis=1,
            )
            v = dot(lt[0], z) + dot(lt[1], z)
            values.append(jnp.concatenate([v[:, :FB], v[:, FB:]], axis=0))
        values = [halves(dot(jnp.concatenate(split(v), axis=1), rr[...])) for v in values]
        scale = jnp.concatenate([inv[...], inv[...]], axis=0)
        values = [v * scale for v in values]
        values = [halves(dot(jnp.concatenate(split(v), axis=1), rrt[...])) for v in values]
        for two, v in zip(pairs, values):
            high, low = [beside(part) for part in split(v)]
            v = (dot(l[0], high) + dot(l[1], high) + dot(l[0], low)).astype(bf16)
            for k, at in enumerate(two):
                for a in range(FA):
                    store(at, a, v[a * 16 : (a + 1) * 16, k * FB : (k + 1) * FB])
        return carry

    lax.fori_loop(0, x.shape[0] // (32 * PAIRS), some, 0)


def whole(a):
    return pl.BlockSpec(a.shape, lambda *_: (0,) * len(a.shape))


def own_kernel(me, partner, x, left, right, eigen, stays, leaves, *ready):
    lower = jnp.bitwise_and(me[0], partner[0, 0]) == 0

    @pl.when(lower)
    def _():
        @pl.when(pl.program_id(0) == 0)
        def _():
            prepare(left, right, eigen, *ready)

        def store(at, a, v):
            out, a = (stays, a) if a < FA // 2 else (leaves, a - FA // 2)
            out[at, a * FB : (a + 1) * FB] = v

        precondition(x, store, *ready)

    @pl.when(jnp.logical_not(lower))
    def _():
        stays[...] = x[:, HALF:]
        leaves[...] = x[:, :HALF]


def own_side(me, partner, x, left, right, eigen):
    step = 32 * PAIRS
    rows = pl.BlockSpec((step, HALF), lambda i: (i, 0))
    shape = jax.ShapeDtypeStruct((ROWS, HALF), bf16)
    return pl.pallas_call(
        own_kernel,
        grid=(ROWS // step,),
        out_shape=(shape, shape),
        in_specs=[SMEM, SMEM, pl.BlockSpec((step, COLS), lambda i: (i, 0))]
        + [whole(a) for a in (left, right, eigen)],
        out_specs=(rows, rows),
        scratch_shapes=PREPARED,
        name="own",
        **params(5 << 30, 4 << 20, 56),
    )(me, partner, x, left, right, eigen)


def shares(v, out):
    for i in range(8):
        first = ((i % 2) * 4 + i // 2) * SHARE
        out[i] = v[first : first + SHARE].astype(out.dtype)


TILE = jax.ShapeDtypeStruct((8, SHARE, ROWS), bf16)


def ordered(tile):
    return tile.reshape(4, 2, SHARE, ROWS)


def both_kernel(arrived, stays, near, far):
    v = dot_t(arrived[...], stays[...]) * SCALE
    shares(v.T, far)
    shares(v, near)


def both_tiles(arrived, stays):
    near, far = pl.pallas_call(
        both_kernel,
        out_shape=(TILE, TILE),
        in_specs=[VMEM, VMEM],
        out_specs=(VMEM, VMEM),
        name="both_tiles",
        **params(2 * ROWS * ROWS * HALF, 4 << 20, 56),
    )(arrived, stays)
    return ordered(near), ordered(far)


def full_kernel(first, stays, second, leaves, out):
    shares((dot_t(first[...], stays[...]) + dot_t(second[...], leaves[...])) * SCALE, out)


def full_tile(first, stays, second, leaves):
    out = pl.pallas_call(
        full_kernel,
        out_shape=TILE,
        in_specs=[VMEM] * 4,
        out_specs=VMEM,
        name="full_tile",
        **params(4 * ROWS * ROWS * HALF, 5 << 20, 56),
    )(first, stays, second, leaves)
    return ordered(out)


def fold_kernel(parts, out):
    for z in range(2):
        four = [parts[y, z].astype(f32) for y in range(4)]
        out[z] = (four[0] + four[1]) + (four[2] + four[3])


def over_y(tile):
    parts = lax.all_to_all(tile, "feat", 0, 0, axis_index_groups=Y_GROUPS)
    return pl.pallas_call(
        fold_kernel,
        out_shape=jax.ShapeDtypeStruct((2, SHARE, ROWS), f32),
        in_specs=[VMEM],
        out_specs=VMEM,
        name="fold",
        **params(0, 4 * parts.size),
    )(parts)


def merge_kernel(z_hi, *refs):
    sums, (keep, send) = refs[:-2], refs[-2:]
    for z, out in ((z_hi[0], keep), (1 - z_hi[0], send)):
        v = sums[0][z]
        for more in sums[1:]:
            v = v + more[z]
        out[...] = v.astype(out.dtype)


def merge(z_hi, near, far):
    sums, shape = [near] if far is None else [near, far], (SHARE, ROWS)
    return pl.pallas_call(
        merge_kernel,
        out_shape=(jax.ShapeDtypeStruct(shape, f32), jax.ShapeDtypeStruct(shape, bf16)),
        in_specs=[SMEM] + [VMEM] * len(sums),
        out_specs=(VMEM, VMEM),
        name="merge",
        **params(0, 4 * SHARE * ROWS * 6),
    )(z_hi, *sums)


def over_z(x):
    return lax.ppermute(x, "feat", [(f, f ^ 4) for f in range(8)])


def swap(level, x):
    return lax.ppermute(x, "blk", [(b, b ^ (1 << level)) for b in range(64)])


def swap_far(level, x):
    return lax.switch(level - 1, [functools.partial(swap, k) for k in range(1, 6)], x)


def by_blocks(level, stays, leaves):
    return over_y(full_tile(swap(0, leaves), stays, swap(0, stays), leaves)), None


def by_halves(level, stays, leaves):
    near, far = both_tiles(swap_far(level, leaves), stays)
    far = over_y(far)
    return over_y(near), swap_far(level, far)


def body(grads, basis_left, basis_right, eigen, partner):
    mask = partner[0, 0]
    blk = lax.axis_index("blk").astype(jnp.int32).reshape(1)
    z_hi = (lax.axis_index("feat") // 4).astype(jnp.int32).reshape(1)
    level = sum((mask >= 1 << k).astype(jnp.int32) for k in range(1, 6))
    stays, leaves = own_side(
        blk, partner, grads, basis_left[0], basis_right[0], eigen.reshape(FA, FB)
    )
    keep, send = lax.cond(
        level == 0,
        lambda *args: merge(z_hi, *by_blocks(*args)),
        lambda *args: merge(z_hi, *by_halves(*args)),
        level,
        stays,
        leaves,
    )
    return (keep + over_z(send)).T[None]


def solution(mesh):
    placed = (P("blk", "feat"), P("feat", None, None), P("feat", None, None), P("feat"), P())
    return jax.shard_map(
        body, mesh=mesh, in_specs=placed, out_specs=P(None, "blk", "feat"), check_vma=False
    )
```

```python
import functools

import jax
import jax.numpy as jnp
from jax import lax
from jax.experimental import pallas as pl
from jax.experimental.pallas import tpu as pltpu
from jax.sharding import PartitionSpec as P

FA = 16
FB = 128
ROWS = 512
COLS = FA * FB
WIDE = 16 * FA
SHARE = 64
PAIRS = 4
HALF = COLS // 2
SCALE = 1.0 / 128.0
Y_GROUPS = [[0, 1, 2, 3], [4, 5, 6, 7]]
VMEM = pl.BlockSpec(memory_space=pltpu.VMEM)
SMEM = pl.BlockSpec(memory_space=pltpu.SMEM)
f32, bf16 = jnp.float32, jnp.bfloat16


def params(flops, moved, grant=28):
    return dict(
        compiler_params=pltpu.CompilerParams(vmem_limit_bytes=grant << 20),
        cost_estimate=pl.CostEstimate(flops=flops, bytes_accessed=moved, transcendentals=0),
    )


def split(v):
    high = v.astype(bf16)
    return high, (v - high.astype(f32)).astype(bf16)


def dot(a, b):
    return jnp.dot(a, b, preferred_element_type=f32)


def dot_t(a, b):
    return lax.dot_general(a, b, (((1,), (1,)), ((), ())), preferred_element_type=f32)


def prepare(left, right, eigen, lt, l, rr, rrt, inv):
    spread = (
        lax.broadcasted_iota(jnp.int32, (WIDE, FA), 0) >> 4
        == lax.broadcasted_iota(jnp.int32, (WIDE, FA), 1)
    ).astype(bf16)
    same = (lax.broadcasted_iota(jnp.int32, (WIDE, WIDE), 0) & 15) == (
        lax.broadcasted_iota(jnp.int32, (WIDE, WIDE), 1) & 15
    )
    for k, v in enumerate(split(left[...])):
        wide = dot_t(dot(spread, v).astype(bf16), spread)
        l[k] = jnp.where(same, wide, 0.0).astype(bf16)
        wide = dot_t(dot_t(spread, v).astype(bf16), spread)
        lt[k] = jnp.where(same, wide, 0.0).astype(bf16)
    for out, basis in ((rr, right[...]), (rrt, right[...].T)):
        for k, v in enumerate(split(basis)):
            out[:FB, k * FB : (k + 1) * FB] = v
            out[FB:, k * FB : (k + 1) * FB] = v
    reciprocal = 1.0 / (eigen[...] + 0.1)
    inv[...] = jnp.broadcast_to(reciprocal[:, None, :], (FA, 16, FB)).reshape(WIDE, FB)


PREPARED = (
    pltpu.VMEM((2, WIDE, WIDE), bf16),
    pltpu.VMEM((2, WIDE, WIDE), bf16),
    pltpu.VMEM((2 * FB, 2 * FB), bf16),
    pltpu.VMEM((2 * FB, 2 * FB), bf16),
    pltpu.VMEM((WIDE, FB), f32),
)


def halves(v):
    return v[:, :FB] + v[:, FB:]


def beside(v):
    return jnp.concatenate([v[:WIDE], v[WIDE:]], axis=1)


def precondition(x, store, lt, l, rr, rrt, inv):
    def some(g, carry):
        pairs = [
            [pl.ds(pl.multiple_of(((g * PAIRS + q) * 2 + k) * 16, 16), 16) for k in range(2)]
            for q in range(PAIRS)
        ]
        values = []
        for two in pairs:
            z = jnp.concatenate(
                [
                    jnp.concatenate([x[at, a * FB : (a + 1) * FB] for a in range(FA)], axis=0)
                    for at in two
                ],
                axis=1,
            )
            v = dot(lt[0], z) + dot(lt[1], z)
            values.append(jnp.concatenate([v[:, :FB], v[:, FB:]], axis=0))
        values = [halves(dot(jnp.concatenate(split(v), axis=1), rr[...])) for v in values]
        scale = jnp.concatenate([inv[...], inv[...]], axis=0)
        values = [v * scale for v in values]
        values = [halves(dot(jnp.concatenate(split(v), axis=1), rrt[...])) for v in values]
        for two, v in zip(pairs, values):
            high, low = [beside(part) for part in split(v)]
            v = (dot(l[0], high) + dot(l[1], high) + dot(l[0], low)).astype(bf16)
            for k, at in enumerate(two):
                for a in range(FA):
                    store(at, a, v[a * 16 : (a + 1) * 16, k * FB : (k + 1) * FB])
        return carry

    lax.fori_loop(0, x.shape[0] // (32 * PAIRS), some, 0)


def whole(a):
    return pl.BlockSpec(a.shape, lambda *_: (0,) * len(a.shape))


def own_kernel(me, partner, x, left, right, eigen, stays, leaves, *ready):
    lower = jnp.bitwise_and(me[0], partner[0, 0]) == 0

    @pl.when(lower)
    def _():
        @pl.when(pl.program_id(0) == 0)
        def _():
            prepare(left, right, eigen, *ready)

        def store(at, a, v):
            out, a = (stays, a) if a < FA // 2 else (leaves, a - FA // 2)
            out[at, a * FB : (a + 1) * FB] = v

        precondition(x, store, *ready)

    @pl.when(jnp.logical_not(lower))
    def _():
        stays[...] = x[:, HALF:]
        leaves[...] = x[:, :HALF]


def own_side(me, partner, x, left, right, eigen):
    step = 32 * PAIRS
    rows = pl.BlockSpec((step, HALF), lambda i: (i, 0))
    shape = jax.ShapeDtypeStruct((ROWS, HALF), bf16)
    return pl.pallas_call(
        own_kernel,
        grid=(ROWS // step,),
        out_shape=(shape, shape),
        in_specs=[SMEM, SMEM, pl.BlockSpec((step, COLS), lambda i: (i, 0))]
        + [whole(a) for a in (left, right, eigen)],
        out_specs=(rows, rows),
        scratch_shapes=PREPARED,
        name="own",
        **params(5 << 30, 4 << 20, 56),
    )(me, partner, x, left, right, eigen)


def shares(v, out):
    rows = v.shape[0] // 8
    for i in range(8):
        first = ((i % 2) * 4 + i // 2) * rows
        out[i] = v[first : first + rows].astype(out.dtype)


TILE = jax.ShapeDtypeStruct((8, SHARE, ROWS), bf16)


def ordered(tile):
    return tile.reshape(4, 2, *tile.shape[1:])


def both_kernel(arrived, stays, near, far):
    v = dot_t(arrived[...], stays[...]) * SCALE
    shares(v.T, far)
    shares(v, near)


def both_tiles(arrived, stays):
    near, far = pl.pallas_call(
        both_kernel,
        out_shape=(TILE, TILE),
        in_specs=[VMEM, VMEM],
        out_specs=(VMEM, VMEM),
        name="both_tiles",
        **params(2 * ROWS * ROWS * HALF, 4 << 20, 56),
    )(arrived, stays)
    return ordered(near), ordered(far)


def full_kernel(first, stays, second, leaves, out):
    shares((dot_t(first[...], stays[...]) + dot_t(second[...], leaves[...])) * SCALE, out)


def full_tile(first, stays, second, leaves):
    out = pl.pallas_call(
        full_kernel,
        out_shape=TILE,
        in_specs=[VMEM] * 4,
        out_specs=VMEM,
        name="full_tile",
        **params(4 * ROWS * ROWS * HALF, 5 << 20, 56),
    )(first, stays, second, leaves)
    return ordered(out)


def fold_kernel(parts, out):
    for z in range(2):
        four = [parts[y, z].astype(f32) for y in range(4)]
        out[z] = (four[0] + four[1]) + (four[2] + four[3])


def over_y(tile):
    parts = lax.all_to_all(tile, "feat", 0, 0, axis_index_groups=Y_GROUPS)
    return pl.pallas_call(
        fold_kernel,
        out_shape=jax.ShapeDtypeStruct(parts.shape[1:], f32),
        in_specs=[VMEM],
        out_specs=VMEM,
        name="fold",
        **params(0, 4 * parts.size),
    )(parts)


def merge_kernel(z_hi, *refs):
    sums, (keep, send) = refs[:-2], refs[-2:]
    for z, out in ((z_hi[0], keep), (1 - z_hi[0], send)):
        v = sums[0][z]
        for more in sums[1:]:
            v = v + more[z]
        out[...] = v.astype(out.dtype)


def merge(z_hi, *sums):
    shape = (SHARE, ROWS)
    return pl.pallas_call(
        merge_kernel,
        out_shape=(jax.ShapeDtypeStruct(shape, f32), jax.ShapeDtypeStruct(shape, bf16)),
        in_specs=[SMEM] + [VMEM] * len(sums),
        out_specs=(VMEM, VMEM),
        name="merge",
        **params(0, 4 * SHARE * ROWS * 6),
    )(z_hi, *sums)


def over_z(x):
    return lax.ppermute(x, "feat", [(f, f ^ 4) for f in range(8)])


def swap(level, x):
    return lax.ppermute(x, "blk", [(b, b ^ (1 << level)) for b in range(64)])


def swap_along(level, x):
    return lax.switch(level - 1, [functools.partial(swap, k) for k in range(1, 6)], x)


def by_blocks(level, z_hi, stays, leaves):
    tile = full_tile(swap(0, leaves), stays, swap(0, stays), leaves)
    return merge(z_hi, over_y(tile))


def by_halves(level, z_hi, stays, leaves):
    near, far = both_tiles(swap_along(level, leaves), stays)
    far = over_y(far)
    return merge(z_hi, over_y(near), swap_along(level, far))


def body(grads, basis_left, basis_right, eigen, partner):
    mask = partner[0, 0]
    blk = lax.axis_index("blk").astype(jnp.int32).reshape(1)
    z_hi = (lax.axis_index("feat") >> 2).astype(jnp.int32).reshape(1)
    level = lax.population_count(mask - 1)
    stays, leaves = own_side(
        blk, partner, grads, basis_left[0], basis_right[0], eigen.reshape(FA, FB)
    )
    keep, send = lax.cond(level == 0, by_blocks, by_halves, level, z_hi, stays, leaves)
    return (keep + over_z(send)).T[None]


def solution(mesh):
    placed = (P("blk", "feat"), P("feat", None, None), P("feat", None, None), P("feat"), P())
    return jax.shard_map(
        body, mesh=mesh, in_specs=placed, out_specs=P(None, "blk", "feat"), check_vma=False
    )
```

```python
import functools

import jax
import jax.numpy as jnp
from jax import lax
from jax.experimental import pallas as pl
from jax.experimental.pallas import tpu as pltpu
from jax.sharding import PartitionSpec as P

FA = 16
FB = 128
ROWS = 512
COLS = FA * FB
WIDE = 16 * FA
SHARE = 64
PAIRS = 4
HALF = COLS // 2
SCALE = 1.0 / 128.0
Y_GROUPS = [[0, 1, 2, 3], [4, 5, 6, 7]]
VMEM = pl.BlockSpec(memory_space=pltpu.VMEM)
SMEM = pl.BlockSpec(memory_space=pltpu.SMEM)
f32, bf16 = jnp.float32, jnp.bfloat16


def params(flops, moved, grant=28):
    return dict(
        compiler_params=pltpu.CompilerParams(vmem_limit_bytes=grant << 20),
        cost_estimate=pl.CostEstimate(flops=flops, bytes_accessed=moved, transcendentals=0),
    )


def split(v):
    high = v.astype(bf16)
    return high, (v - high.astype(f32)).astype(bf16)


def dot(a, b):
    return jnp.dot(a, b, preferred_element_type=f32)


def dot_t(a, b):
    return lax.dot_general(a, b, (((1,), (1,)), ((), ())), preferred_element_type=f32)


def prepare(left, right, eigen, lt, l, rr, rrt, inv):
    spread = (
        lax.broadcasted_iota(jnp.int32, (WIDE, FA), 0) >> 4
        == lax.broadcasted_iota(jnp.int32, (WIDE, FA), 1)
    ).astype(bf16)
    same = (lax.broadcasted_iota(jnp.int32, (WIDE, WIDE), 0) & 15) == (
        lax.broadcasted_iota(jnp.int32, (WIDE, WIDE), 1) & 15
    )
    for k, v in enumerate(split(left[...])):
        wide = dot_t(dot(spread, v).astype(bf16), spread)
        l[k] = jnp.where(same, wide, 0.0).astype(bf16)
        wide = dot_t(dot_t(spread, v).astype(bf16), spread)
        lt[k] = jnp.where(same, wide, 0.0).astype(bf16)
    for out, basis in ((rr, right[...]), (rrt, right[...].T)):
        for k, v in enumerate(split(basis)):
            out[:FB, k * FB : (k + 1) * FB] = v
            out[FB:, k * FB : (k + 1) * FB] = v
    reciprocal = 1.0 / (eigen[...] + 0.1)
    inv[...] = jnp.broadcast_to(reciprocal[:, None, :], (FA, 16, FB)).reshape(WIDE, FB)


PREPARED = (
    pltpu.VMEM((2, WIDE, WIDE), bf16),
    pltpu.VMEM((2, WIDE, WIDE), bf16),
    pltpu.VMEM((2 * FB, 2 * FB), bf16),
    pltpu.VMEM((2 * FB, 2 * FB), bf16),
    pltpu.VMEM((WIDE, FB), f32),
)


def halves(v):
    return v[:, :FB] + v[:, FB:]


def beside(v):
    return jnp.concatenate([v[:WIDE], v[WIDE:]], axis=1)


def precondition(x, store, lt, l, rr, rrt, inv):
    def some(g, carry):
        pairs = [
            [pl.ds(pl.multiple_of(((g * PAIRS + q) * 2 + k) * 16, 16), 16) for k in range(2)]
            for q in range(PAIRS)
        ]
        values = []
        for two in pairs:
            z = jnp.concatenate(
                [
                    jnp.concatenate([x[at, a * FB : (a + 1) * FB] for a in range(FA)], axis=0)
                    for at in two
                ],
                axis=1,
            )
            v = dot(lt[0], z) + dot(lt[1], z)
            values.append(jnp.concatenate([v[:, :FB], v[:, FB:]], axis=0))
        values = [halves(dot(jnp.concatenate(split(v), axis=1), rr[...])) for v in values]
        scale = jnp.concatenate([inv[...], inv[...]], axis=0)
        values = [v * scale for v in values]
        values = [halves(dot(jnp.concatenate(split(v), axis=1), rrt[...])) for v in values]
        for two, v in zip(pairs, values):
            high, low = [beside(part) for part in split(v)]
            v = (dot(l[0], high) + dot(l[1], high) + dot(l[0], low)).astype(bf16)
            for k, at in enumerate(two):
                for a in range(FA):
                    store(at, a, v[a * 16 : (a + 1) * 16, k * FB : (k + 1) * FB])
        return carry

    lax.fori_loop(0, x.shape[0] // (32 * PAIRS), some, 0)


def whole(a):
    return pl.BlockSpec(a.shape, lambda *_: (0,) * len(a.shape))


def own_kernel(me, partner, x, left, right, eigen, stays, leaves, *ready):
    lower = jnp.bitwise_and(me[0], partner[0, 0]) == 0

    @pl.when(lower)
    def _():
        @pl.when(pl.program_id(0) == 0)
        def _():
            prepare(left, right, eigen, *ready)

        def store(at, a, v):
            out, a = (stays, a) if a < FA // 2 else (leaves, a - FA // 2)
            out[at, a * FB : (a + 1) * FB] = v

        precondition(x, store, *ready)

    @pl.when(jnp.logical_not(lower))
    def _():
        stays[...] = x[:, HALF:]
        leaves[...] = x[:, :HALF]


def own_side(me, partner, x, left, right, eigen):
    step = 32 * PAIRS
    rows = pl.BlockSpec((step, HALF), lambda i: (i, 0))
    shape = jax.ShapeDtypeStruct((ROWS, HALF), bf16)
    return pl.pallas_call(
        own_kernel,
        grid=(ROWS // step,),
        out_shape=(shape, shape),
        in_specs=[SMEM, SMEM, pl.BlockSpec((step, COLS), lambda i: (i, 0))]
        + [whole(a) for a in (left, right, eigen)],
        out_specs=(rows, rows),
        scratch_shapes=PREPARED,
        name="own",
        **params(5 << 30, 4 << 20, 56),
    )(me, partner, x, left, right, eigen)


def shares(v, out):
    rows = v.shape[0] // 8
    for i in range(8):
        first = ((i % 2) * 4 + i // 2) * rows
        out[i] = v[first : first + rows].astype(out.dtype)


TILE = jax.ShapeDtypeStruct((8, SHARE, ROWS), bf16)


def ordered(tile):
    return tile.reshape(4, 2, *tile.shape[1:])


def both_kernel(y, arrived, stays, near, far, near_own, far_own, held):
    v = dot_t(arrived[...], stays[...]) * SCALE
    for product, out, own in ((v.T, far, far_own), (v, near, near_own)):
        held[...] = product
        for z in range(2):
            first = (z * 4 + y[0]) * SHARE
            own[z] = held[pl.ds(pl.multiple_of(first, SHARE), SHARE)]
        shares(product, out)


def both_tiles(y, arrived, stays):
    own = jax.ShapeDtypeStruct((2, SHARE, ROWS), f32)
    near, far, near_own, far_own = pl.pallas_call(
        both_kernel,
        out_shape=(TILE, TILE, own, own),
        in_specs=[SMEM, VMEM, VMEM],
        out_specs=(VMEM,) * 4,
        scratch_shapes=[pltpu.VMEM((ROWS, ROWS), f32)],
        name="both_tiles",
        **params(2 * ROWS * ROWS * HALF, 4 << 20, 56),
    )(y, arrived, stays)
    return (ordered(near), near_own), (ordered(far), far_own)


def add_kernel(y, parts, own, out):
    for z in range(2):
        v = own[z]
        for k in range(4):
            part = parts[k, z].astype(f32)
            v = v + jnp.where(y[0] == k, jnp.zeros_like(part), part)
        out[z] = v.astype(out.dtype)


def over_others(y, tile, own, kind):
    parts = lax.all_to_all(tile, "feat", 0, 0, axis_index_groups=Y_GROUPS)
    return pl.pallas_call(
        add_kernel,
        out_shape=jax.ShapeDtypeStruct(own.shape, kind),
        in_specs=[SMEM, VMEM, VMEM],
        out_specs=VMEM,
        name="add",
        **params(0, 4 * parts.size),
    )(y, parts, own)


def full_kernel(first, stays, second, leaves, out):
    shares((dot_t(first[...], stays[...]) + dot_t(second[...], leaves[...])) * SCALE, out)


def full_tile(first, stays, second, leaves):
    out = pl.pallas_call(
        full_kernel,
        out_shape=TILE,
        in_specs=[VMEM] * 4,
        out_specs=VMEM,
        name="full_tile",
        **params(4 * ROWS * ROWS * HALF, 5 << 20, 56),
    )(first, stays, second, leaves)
    return ordered(out)


def fold_kernel(parts, out):
    for z in range(2):
        four = [parts[y, z].astype(f32) for y in range(4)]
        out[z] = (four[0] + four[1]) + (four[2] + four[3])


def over_y(tile):
    parts = lax.all_to_all(tile, "feat", 0, 0, axis_index_groups=Y_GROUPS)
    return pl.pallas_call(
        fold_kernel,
        out_shape=jax.ShapeDtypeStruct(parts.shape[1:], f32),
        in_specs=[VMEM],
        out_specs=VMEM,
        name="fold",
        **params(0, 4 * parts.size),
    )(parts)


def merge_kernel(z_hi, *refs):
    sums, (keep, send) = refs[:-2], refs[-2:]
    for z, out in ((z_hi[0], keep), (1 - z_hi[0], send)):
        v = sums[0][z]
        for more in sums[1:]:
            v = v + more[z].astype(f32)
        out[...] = v.astype(out.dtype)


def merge(z_hi, *sums):
    shape = (SHARE, ROWS)
    return pl.pallas_call(
        merge_kernel,
        out_shape=(jax.ShapeDtypeStruct(shape, f32), jax.ShapeDtypeStruct(shape, bf16)),
        in_specs=[SMEM] + [VMEM] * len(sums),
        out_specs=(VMEM, VMEM),
        name="merge",
        **params(0, 4 * SHARE * ROWS * 6),
    )(z_hi, *sums)


def over_z(x):
    return lax.ppermute(x, "feat", [(f, f ^ 4) for f in range(8)])


def swap(level, x):
    return lax.ppermute(x, "blk", [(b, b ^ (1 << level)) for b in range(64)])


def swap_along(level, x):
    return lax.switch(level - 1, [functools.partial(swap, k) for k in range(1, 6)], x)


def by_blocks(level, z_hi, stays, leaves):
    tile = full_tile(swap(0, leaves), stays, swap(0, stays), leaves)
    return merge(z_hi, over_y(tile))


def by_halves(level, z_hi, stays, leaves):
    y = (lax.axis_index("feat") & 3).astype(jnp.int32).reshape(1)
    near, far = both_tiles(y, swap_along(level, leaves), stays)
    far = over_others(y, *far, bf16)
    return merge(z_hi, over_others(y, *near, f32), swap_along(level, far))


def body(grads, basis_left, basis_right, eigen, partner):
    mask = partner[0, 0]
    blk = lax.axis_index("blk").astype(jnp.int32).reshape(1)
    z_hi = (lax.axis_index("feat") >> 2).astype(jnp.int32).reshape(1)
    level = lax.population_count(mask - 1)
    stays, leaves = own_side(
        blk, partner, grads, basis_left[0], basis_right[0], eigen.reshape(FA, FB)
    )
    keep, send = lax.cond(level == 0, by_blocks, by_halves, level, z_hi, stays, leaves)
    return (keep + over_z(send)).T[None]


def solution(mesh):
    placed = (P("blk", "feat"), P("feat", None, None), P("feat", None, None), P("feat"), P())
    return jax.shard_map(
        body, mesh=mesh, in_specs=placed, out_specs=P(None, "blk", "feat"), check_vma=False
    )
```

```python
import functools

import jax
import jax.numpy as jnp
from jax import lax
from jax.experimental import pallas as pl
from jax.experimental.pallas import tpu as pltpu
from jax.sharding import PartitionSpec as P

FA = 16
FB = 128
ROWS = 512
COLS = FA * FB
WIDE = 16 * FA
SHARE = 64
PAIRS = 8
HALF = COLS // 2
SCALE = 1.0 / 128.0
Y_GROUPS = [[0, 1, 2, 3], [4, 5, 6, 7]]
VMEM = pl.BlockSpec(memory_space=pltpu.VMEM)
SMEM = pl.BlockSpec(memory_space=pltpu.SMEM)
f32, bf16 = jnp.float32, jnp.bfloat16


def params(flops, moved, grant=28):
    return dict(
        compiler_params=pltpu.CompilerParams(vmem_limit_bytes=grant << 20),
        cost_estimate=pl.CostEstimate(flops=flops, bytes_accessed=moved, transcendentals=0),
    )


def split(v):
    high = v.astype(bf16)
    return high, (v - high.astype(f32)).astype(bf16)


def dot(a, b):
    return jnp.dot(a, b, preferred_element_type=f32)


def dot_t(a, b):
    return lax.dot_general(a, b, (((1,), (1,)), ((), ())), preferred_element_type=f32)


def prepare(left, right, eigen, lt, l, rr, rrt, inv):
    spread = (
        lax.broadcasted_iota(jnp.int32, (WIDE, FA), 0) >> 4
        == lax.broadcasted_iota(jnp.int32, (WIDE, FA), 1)
    ).astype(bf16)
    same = (lax.broadcasted_iota(jnp.int32, (WIDE, WIDE), 0) & 15) == (
        lax.broadcasted_iota(jnp.int32, (WIDE, WIDE), 1) & 15
    )
    for k, v in enumerate(split(left[...])):
        wide = dot_t(dot(spread, v).astype(bf16), spread)
        l[k] = jnp.where(same, wide, 0.0).astype(bf16)
        wide = dot_t(dot_t(spread, v).astype(bf16), spread)
        lt[k] = jnp.where(same, wide, 0.0).astype(bf16)
    for out, basis in ((rr, right[...]), (rrt, right[...].T)):
        for k, v in enumerate(split(basis)):
            out[:FB, k * FB : (k + 1) * FB] = v
            out[FB:, k * FB : (k + 1) * FB] = v
    reciprocal = 1.0 / (eigen[...] + 0.1)
    inv[...] = jnp.broadcast_to(reciprocal[:, None, :], (FA, 16, FB)).reshape(WIDE, FB)


PREPARED = (
    pltpu.VMEM((2, WIDE, WIDE), bf16),
    pltpu.VMEM((2, WIDE, WIDE), bf16),
    pltpu.VMEM((2 * FB, 2 * FB), bf16),
    pltpu.VMEM((2 * FB, 2 * FB), bf16),
    pltpu.VMEM((WIDE, FB), f32),
)


def halves(v):
    return v[:, :FB] + v[:, FB:]


def beside(v):
    return jnp.concatenate([v[:WIDE], v[WIDE:]], axis=1)


def precondition(x, store, lt, l, rr, rrt, inv):
    def some(g, carry):
        pairs = [
            [pl.ds(pl.multiple_of(((g * PAIRS + q) * 2 + k) * 16, 16), 16) for k in range(2)]
            for q in range(PAIRS)
        ]
        values = []
        for two in pairs:
            z = jnp.concatenate(
                [
                    jnp.concatenate([x[at, a * FB : (a + 1) * FB] for a in range(FA)], axis=0)
                    for at in two
                ],
                axis=1,
            )
            v = dot(lt[0], z) + dot(lt[1], z)
            values.append(jnp.concatenate([v[:, :FB], v[:, FB:]], axis=0))
        values = [halves(dot(jnp.concatenate(split(v), axis=1), rr[...])) for v in values]
        scale = jnp.concatenate([inv[...], inv[...]], axis=0)
        values = [v * scale for v in values]
        values = [halves(dot(jnp.concatenate(split(v), axis=1), rrt[...])) for v in values]
        for two, v in zip(pairs, values):
            high, low = [beside(part) for part in split(v)]
            v = (dot(l[0], high) + dot(l[1], high) + dot(l[0], low)).astype(bf16)
            for k, at in enumerate(two):
                for a in range(FA):
                    store(at, a, v[a * 16 : (a + 1) * 16, k * FB : (k + 1) * FB])
        return carry

    lax.fori_loop(0, x.shape[0] // (32 * PAIRS), some, 0)


def whole(a):
    return pl.BlockSpec(a.shape, lambda *_: (0,) * len(a.shape))


def own_kernel(me, partner, x, left, right, eigen, stays, leaves, *ready):
    lower = jnp.bitwise_and(me[0], partner[0, 0]) == 0

    @pl.when(lower)
    def _():
        @pl.when(pl.program_id(0) == 0)
        def _():
            prepare(left, right, eigen, *ready)

        def store(at, a, v):
            out, a = (stays, a) if a < FA // 2 else (leaves, a - FA // 2)
            out[at, a * FB : (a + 1) * FB] = v

        precondition(x, store, *ready)

    @pl.when(jnp.logical_not(lower))
    def _():
        stays[...] = x[:, HALF:]
        leaves[...] = x[:, :HALF]


def own_side(me, partner, x, left, right, eigen):
    step = 32 * PAIRS
    rows = pl.BlockSpec((step, HALF), lambda i: (i, 0))
    shape = jax.ShapeDtypeStruct((ROWS, HALF), bf16)
    return pl.pallas_call(
        own_kernel,
        grid=(ROWS // step,),
        out_shape=(shape, shape),
        in_specs=[SMEM, SMEM, pl.BlockSpec((step, COLS), lambda i: (i, 0))]
        + [whole(a) for a in (left, right, eigen)],
        out_specs=(rows, rows),
        scratch_shapes=PREPARED,
        name="own",
        **params(5 << 30, 4 << 20, 56),
    )(me, partner, x, left, right, eigen)


def shares(v, out):
    rows = v.shape[0] // 8
    for i in range(8):
        first = ((i % 2) * 4 + i // 2) * rows
        out[i] = v[first : first + rows].astype(out.dtype)


TILE = jax.ShapeDtypeStruct((8, SHARE, ROWS), bf16)


def ordered(tile):
    return tile.reshape(4, 2, *tile.shape[1:])


def both_kernel(y, arrived, stays, near, far, near_own, far_own, held):
    v = dot_t(arrived[...], stays[...]) * SCALE
    for product, out, own in ((v.T, far, far_own), (v, near, near_own)):
        held[...] = product
        for z in range(2):
            first = (z * 4 + y[0]) * SHARE
            own[z] = held[pl.ds(pl.multiple_of(first, SHARE), SHARE)]
        shares(product, out)


def both_tiles(y, arrived, stays):
    own = jax.ShapeDtypeStruct((2, SHARE, ROWS), f32)
    near, far, near_own, far_own = pl.pallas_call(
        both_kernel,
        out_shape=(TILE, TILE, own, own),
        in_specs=[SMEM, VMEM, VMEM],
        out_specs=(VMEM,) * 4,
        scratch_shapes=[pltpu.VMEM((ROWS, ROWS), f32)],
        name="both_tiles",
        **params(2 * ROWS * ROWS * HALF, 4 << 20, 56),
    )(y, arrived, stays)
    return (ordered(near), near_own), (ordered(far), far_own)


def add_kernel(y, parts, own, out):
    for z in range(2):
        v = own[z]
        for k in range(4):
            part = parts[k, z].astype(f32)
            v = v + jnp.where(y[0] == k, jnp.zeros_like(part), part)
        out[z] = v.astype(out.dtype)


def over_others(y, tile, own, kind):
    parts = lax.all_to_all(tile, "feat", 0, 0, axis_index_groups=Y_GROUPS)
    return pl.pallas_call(
        add_kernel,
        out_shape=jax.ShapeDtypeStruct(own.shape, kind),
        in_specs=[SMEM, VMEM, VMEM],
        out_specs=VMEM,
        name="add",
        **params(0, 4 * parts.size),
    )(y, parts, own)


def full_kernel(first, stays, second, leaves, out):
    shares((dot_t(first[...], stays[...]) + dot_t(second[...], leaves[...])) * SCALE, out)


def full_tile(first, stays, second, leaves):
    out = pl.pallas_call(
        full_kernel,
        out_shape=TILE,
        in_specs=[VMEM] * 4,
        out_specs=VMEM,
        name="full_tile",
        **params(4 * ROWS * ROWS * HALF, 5 << 20, 56),
    )(first, stays, second, leaves)
    return ordered(out)


def fold_kernel(parts, out):
    for z in range(2):
        four = [parts[y, z].astype(f32) for y in range(4)]
        out[z] = (four[0] + four[1]) + (four[2] + four[3])


def over_y(tile):
    parts = lax.all_to_all(tile, "feat", 0, 0, axis_index_groups=Y_GROUPS)
    return pl.pallas_call(
        fold_kernel,
        out_shape=jax.ShapeDtypeStruct(parts.shape[1:], f32),
        in_specs=[VMEM],
        out_specs=VMEM,
        name="fold",
        **params(0, 4 * parts.size),
    )(parts)


def merge_kernel(z_hi, *refs):
    sums, (keep, send) = refs[:-2], refs[-2:]
    for z, out in ((z_hi[0], keep), (1 - z_hi[0], send)):
        v = sums[0][z]
        for more in sums[1:]:
            v = v + more[z].astype(f32)
        out[...] = v.astype(out.dtype)


def merge(z_hi, *sums):
    shape = (SHARE, ROWS)
    return pl.pallas_call(
        merge_kernel,
        out_shape=(jax.ShapeDtypeStruct(shape, f32), jax.ShapeDtypeStruct(shape, bf16)),
        in_specs=[SMEM] + [VMEM] * len(sums),
        out_specs=(VMEM, VMEM),
        name="merge",
        **params(0, 4 * SHARE * ROWS * 6),
    )(z_hi, *sums)


def over_z(x):
    return lax.ppermute(x, "feat", [(f, f ^ 4) for f in range(8)])


def swap(level, x):
    return lax.ppermute(x, "blk", [(b, b ^ (1 << level)) for b in range(64)])


def swap_along(level, x):
    return lax.switch(level - 1, [functools.partial(swap, k) for k in range(1, 6)], x)


def by_blocks(level, z_hi, stays, leaves):
    tile = full_tile(swap(0, leaves), stays, swap(0, stays), leaves)
    return merge(z_hi, over_y(tile))


def by_halves(level, z_hi, stays, leaves):
    y = (lax.axis_index("feat") & 3).astype(jnp.int32).reshape(1)
    near, far = both_tiles(y, swap_along(level, leaves), stays)
    far = over_others(y, *far, bf16)
    return merge(z_hi, over_others(y, *near, f32), swap_along(level, far))


def body(grads, basis_left, basis_right, eigen, partner):
    mask = partner[0, 0]
    blk = lax.axis_index("blk").astype(jnp.int32).reshape(1)
    z_hi = (lax.axis_index("feat") >> 2).astype(jnp.int32).reshape(1)
    level = lax.population_count(mask - 1)
    stays, leaves = own_side(
        blk, partner, grads, basis_left[0], basis_right[0], eigen.reshape(FA, FB)
    )
    keep, send = lax.cond(level == 0, by_blocks, by_halves, level, z_hi, stays, leaves)
    return (keep + over_z(send)).T[None]


def solution(mesh):
    placed = (P("blk", "feat"), P("feat", None, None), P("feat", None, None), P("feat"), P())
    return jax.shard_map(
        body, mesh=mesh, in_specs=placed, out_specs=P(None, "blk", "feat"), check_vma=False
    )
```
